32 devices in a mesh: dp: 8 (over y, x, core), expert: 4 (over z).
Axes of the slice: x: 2, y: 2, z: 4, core: 2. Of those that a mesh axis runs over, the one named last changes fastest.
Arguments:
- hidden_in: bfloat16 [16384, 1024], P(('dp', 'expert')), may hold values from -6 to 6
- norm1_gain: bfloat16 [1024], P(('dp', 'expert')), may hold values from 0.5 to 1.5
- w_query: bfloat16 [1024, 1024], P(('dp', 'expert')), may hold values from -0.1875 to 0.1875
- w_key: bfloat16 [1024, 512], P(('dp', 'expert')), may hold values from -0.1875 to 0.1875
- w_value: bfloat16 [1024, 512], P(('dp', 'expert')), may hold values from -0.1875 to 0.1875
- w_out: bfloat16 [1024, 1024], P(('dp', 'expert')), may hold values from -2 to 2
- norm2_gain: bfloat16 [1024], P(('dp', 'expert')), may hold values from 0.5 to 1.5
- w_router: bfloat16 [1024, 32], P(('dp', 'expert')), may hold values from -0.09375 to 0.09375
- w_gate: bfloat16 [32, 1024, 512], P('expert', 'dp'), may hold values from -0.1875 to 0.1875
- w_up: bfloat16 [32, 1024, 512], P('expert', 'dp'), may hold values from -0.1875 to 0.1875
- w_down: bfloat16 [32, 512, 1024], P('expert', None, 'dp'), may hold values from -1 to 1
- expert_ids: int32 [16384, 8], P(('dp', 'expert')), may hold values from 0 to 31, all different within a row; in each aligned block of 512 rows (0 to 511, 512 to 1023, ...) at most 152 rows name the same one
- out_grad: bfloat16 [16384, 1024], P(('dp', 'expert')), may hold values from -6 to 6
Outputs:
- layer_out: bfloat16 [16384, 1024], P(('dp', 'expert'))
- in_grad: bfloat16 [16384, 1024], P(('dp', 'expert'))
- grad_norm1: float32 [1024], P(('dp', 'expert'))
- grad_query: float32 [1024, 1024], P(('dp', 'expert'))
- grad_key: float32 [1024, 512], P(('dp', 'expert'))
- grad_value: float32 [1024, 512], P(('dp', 'expert'))
- grad_out: float32 [1024, 1024], P(('dp', 'expert'))
- grad_norm2: float32 [1024], P(('dp', 'expert'))
- grad_router: float32 [1024, 32], P(('dp', 'expert'))
- grad_gate: float32 [32, 1024, 512], P('expert', 'dp')
- grad_up: float32 [32, 1024, 512], P('expert', 'dp')
- grad_down: float32 [32, 512, 1024], P('expert', None, 'dp')
The draws below stay inside these ranges and needn't reach their ends.
Inputs may be any that keep to these rules, and one draw needn't show every extreme that they name: `expert_ids`: each row names 8 different experts; among the 512 rows of one device no expert is named more than 152 times, a bound that some block reaches.
All inputs are finite; a program needn't handle non-finite values.
Results may differ from the reference program's by a relative error of at most 0.015.
Values may be sent and summed in bfloat16 or wider, within the bound.
A program may use at most 256 MiB of HBM per device.

```python
import math
import jax
import jax.numpy as jnp
import numpy as np
from jax import lax

D = 1024
HEADS = 16
KV_HEADS = 8
HEAD_DIM = 64
EXPERTS = 32
TOPK = 8
FF_EXP = 512
TOK_DEV = 512
CAP = 152
TOKENS = 16384


def block_scale(key, extent, cuts, least, largest):
    level, own = 1.0, jax.random.fold_in(key, 6)
    for dim, parts in cuts:
        steps = jnp.exp(jax.random.uniform(jax.random.fold_in(own, dim), (parts,), jnp.float32, least / len(cuts), largest / len(cuts)))
        level = level * jnp.repeat(steps, extent[dim] // parts).reshape([-1 if axis == dim else 1 for axis in range(len(extent))])
    return level


def deal_out(rng, own, number, rows, amount, top, limit, skew):
    ranking = jax.random.permutation(rng, amount)
    crowded, common = load_shares(amount, rows * top, limit, skew, True), load_shares(amount, rows * top, limit, skew, False)
    places = jnp.arange(amount)

    def named(lengths, rotation):
        used = int((lengths > 0).sum())
        fixed = max(1, used // 4)
        passed = fixed + (places - fixed + rotation * (used - fixed)) % max(1, amount - fixed)
        return jnp.zeros((amount,), jnp.int32).at[ranking[jnp.where(places < fixed, places, passed)]].set(jnp.asarray(lengths, jnp.int32))

    lengths = jnp.where(number % 4 == 0, named(crowded, number // 4), named(common, number - number // 4 - 1))
    mixed = jax.random.permutation(jax.random.fold_in(own, 3), amount)
    donor, taker = mixed[0:amount // 2 * 2:2], mixed[1:amount // 2 * 2:2]
    margin = jnp.minimum(lengths[donor] - 1, limit - lengths[taker]) // 2
    margin = jnp.where((donor == ranking[0]) | (taker == ranking[0]) | (lengths[taker] == 0), 0, jnp.maximum(margin, 0))
    passed = jax.random.randint(jax.random.fold_in(own, 4), (amount // 2,), 0, 1 << 20) % (margin + 1)
    lengths = lengths.at[donor].add(-passed).at[taker].add(passed)
    items = jnp.searchsorted(jnp.cumsum(lengths), jnp.arange(rows * top), side="right").astype(jnp.int32)
    grid = items.reshape(top, rows).T
    grid = grid[jax.random.permutation(jax.random.fold_in(own, 1), rows)]
    rotation = jax.random.randint(jax.random.fold_in(own, 2), (rows, 1), 0, top)
    return jnp.take_along_axis(grid, (jnp.arange(top)[None, :] + rotation) % top, axis=1)


def load_shares(count, total, bound, skew, full):
    portions = [(1 << 20) // math.isqrt(rank ** skew) + 1 for rank in range(1, count + 1)]
    largest = bound if full else min(bound, max(-(-total // count), total * portions[0] // sum(portions)))
    least = 1 if total - largest >= count - 1 else 0
    counts, spare = [largest] + [least] * (count - 1), total - largest - least * (count - 1)
    while spare > 0:
        candidates = [i for i in range(1, count) if counts[i] < largest] or [i for i in range(1, count) if counts[i] < bound]
        pool, left = sum([portions[i] for i in candidates]), spare
        for i in candidates:
            extra = min(bound - counts[i], max(1, left * portions[i] // pool), spare)
            counts[i] = counts[i] + extra
            spare = spare - extra
    return np.array(counts)


def bell_draw(rng, extent, scale, most, cuts=(), kind=jnp.bfloat16):
    values = scale * jax.random.normal(rng, extent, jnp.float32)
    if cuts:
        values = values * block_scale(rng, extent, cuts, -0.22, 0.18)
    return jnp.clip(values, -most, most).astype(kind)


def setup_inputs(seed: int = 0) -> dict:
    seeds = jax.random.split(jax.random.key(seed), 14)
    hidden_in = bell_draw(seeds[0], (TOKENS, D), 1.0, 6.0, ((0, 32),))
    norm1_gain = jnp.clip(1.0 + 0.1 * jax.random.normal(seeds[1], (D,), jnp.float32), 0.5, 1.5).astype(jnp.bfloat16)
    w_query = bell_draw(seeds[2], (D, HEADS * HEAD_DIM), D ** -0.5, 0.1875, ((0, 32),))
    w_key = bell_draw(seeds[3], (D, KV_HEADS * HEAD_DIM), D ** -0.5, 0.1875, ((0, 32),))
    w_value = bell_draw(seeds[4], (D, KV_HEADS * HEAD_DIM), D ** -0.5, 0.1875, ((0, 32),))
    w_out = bell_draw(seeds[5], (HEADS * HEAD_DIM, D), (HEADS * HEAD_DIM // 128) ** -0.5, 2.0, ((0, 32),))
    norm2_gain = jnp.clip(1.0 + 0.1 * jax.random.normal(seeds[6], (D,), jnp.float32), 0.5, 1.5).astype(jnp.bfloat16)
    w_router = bell_draw(seeds[7], (D, EXPERTS), (4 * D) ** -0.5, 0.09375, ((0, 32),))
    w_gate = bell_draw(seeds[8], (EXPERTS, D, FF_EXP), D ** -0.5, 0.1875, ((0, 4), (1, 8)))
    w_up = bell_draw(seeds[9], (EXPERTS, D, FF_EXP), D ** -0.5, 0.1875, ((0, 4), (1, 8)))
    w_down = bell_draw(seeds[10], (EXPERTS, FF_EXP, D), (FF_EXP // 16) ** -0.5, 1.0, ((0, 4), (2, 8)))
    expert_ids_keys = jax.random.split(jax.random.fold_in(seeds[11], 1), TOKENS // TOK_DEV)
    expert_ids_turns = jax.random.permutation(jax.random.fold_in(seeds[11], 3), TOKENS // TOK_DEV)
    expert_ids = jax.vmap(lambda own, number: deal_out(jax.random.fold_in(seeds[11], 2), own, number, TOK_DEV, EXPERTS, TOPK, CAP, 1))(expert_ids_keys, expert_ids_turns).reshape((TOKENS, TOPK))
    out_grad = bell_draw(seeds[12], (TOKENS, D), 1.0, 6.0, ((0, 32),))
    return dict(hidden_in=hidden_in, norm1_gain=norm1_gain, w_query=w_query, w_key=w_key, w_value=w_value, w_out=w_out, norm2_gain=norm2_gain, w_router=w_router, w_gate=w_gate, w_up=w_up, w_down=w_down, expert_ids=expert_ids, out_grad=out_grad)


@jax.custom_vjp
def low(v):
    return lax.optimization_barrier(v.astype(jnp.bfloat16)).astype(jnp.float32)

@jax.custom_vjp
def low_back(v):
    return v

def low_keep(v):
    return (low(v), None)

def low_pass(kept, grad):
    return (grad,)

def back_keep(v):
    return (v, None)

def back_low(kept, grad):
    return (low(grad),)
low.defvjp(low_keep, low_pass)
low_back.defvjp(back_keep, back_low)
EPSILON = 1e-06
HIGHEST = lax.Precision.HIGHEST

def rope_tables(length, head_width):
    half_width = head_width // 2
    ladder = jnp.arange(half_width, dtype=jnp.float32) * (2.0 / head_width)
    inverse = jnp.exp(-math.log(10000.0) * ladder)
    angles = jnp.arange(length, dtype=jnp.float32)[:, None] * inverse[None, :]
    return (jnp.cos(angles), jnp.sin(angles))

def rotate(values, cosine, sine_table):
    half_width = values.shape[-1] // 2
    first_half = values[..., :half_width]
    second = values[..., half_width:]
    cos_rows = cosine[:, None, :]
    sin_rows = sine_table[:, None, :]
    return jnp.concatenate([first_half * cos_rows - second * sin_rows, second * cos_rows + first_half * sin_rows], axis=-1)

def slot_table(routes):
    flat_ids = routes.reshape(-1)
    row_count = flat_ids.shape[0]
    hit_table = (flat_ids[:, None] == jnp.arange(EXPERTS, dtype=jnp.int32)[None, :]).astype(jnp.int32)
    before = jnp.cumsum(hit_table, axis=0) - hit_table
    slot_rank = lax.optimization_barrier(jnp.sum(before * hit_table, axis=1))
    position = (flat_ids * CAP + slot_rank).astype(jnp.int32)
    table = jnp.full((EXPERTS * CAP,), row_count, jnp.int32).at[position].set(jnp.arange(row_count, dtype=jnp.int32))
    return (position, table)

def rms_norm(values, gain):
    scale_rows = lax.rsqrt(lax.optimization_barrier(jnp.mean(values * values, axis=-1, keepdims=True)) + EPSILON)
    return values * scale_rows * gain

def matmul(left, right):
    return jnp.dot(left, right, precision=HIGHEST)

def attend(queries, keys, values_in):
    length = queries.shape[0]
    block_rows = min(512, length)
    blocks = length // block_rows
    group = HEADS // KV_HEADS
    scale = 1.0 / math.sqrt(HEAD_DIM)
    shaped = queries.reshape(blocks, block_rows, KV_HEADS, group, HEAD_DIM)
    key_pos = jnp.arange(length, dtype=jnp.int32)

    def one_block(operands):
        query_block, start = operands
        scores = jnp.einsum('qgrd,kgd->grqk', query_block, keys, precision=HIGHEST) * scale
        query_pos = start + jnp.arange(block_rows, dtype=jnp.int32)
        scores = jnp.where(key_pos[None, :] <= query_pos[:, None], scores, -1e+30)
        scores = low_back(scores)
        top_score = lax.optimization_barrier(jnp.max(scores, axis=-1, keepdims=True))
        log_total = top_score + jnp.log(lax.optimization_barrier(jnp.sum(jnp.exp(scores - top_score), axis=-1, keepdims=True)))
        weights = low(jnp.exp(scores - log_total))
        return jnp.einsum('grqk,kgd->qgrd', weights, values_in, precision=HIGHEST)
    starts = (jnp.arange(blocks, dtype=jnp.int32) * block_rows).astype(jnp.int32)
    result = lax.map(jax.checkpoint(one_block), (shaped, starts))
    return result.reshape(length, HEADS * HEAD_DIM)

def layer(inputs, gain_one, query_w, key_w, value_w, out_w, gain_two, router_w, gate_w, up_w, down_w, routes):
    length = inputs.shape[0]
    cosine, sine_table = rope_tables(length, HEAD_DIM)
    normed = low(rms_norm(inputs, gain_one))
    queries = low_back(matmul(normed, query_w)).reshape(length, HEADS, HEAD_DIM)
    keys = low_back(matmul(normed, key_w)).reshape(length, KV_HEADS, HEAD_DIM)
    values_in = low(low_back(matmul(normed, value_w))).reshape(length, KV_HEADS, HEAD_DIM)
    queries = low(rotate(queries, cosine, sine_table))
    keys = low(rotate(keys, cosine, sine_table))
    attended = low_back(low(attend(queries, keys, values_in)))
    middle = inputs + low_back(matmul(attended, out_w))
    normed_two = low(rms_norm(middle, gain_two))
    logits = low_back(matmul(normed_two, router_w))
    hit_table = (routes[:, :, None] == jnp.arange(EXPERTS, dtype=jnp.int32)[None, None, :]).astype(jnp.float32)
    picked = lax.optimization_barrier(jnp.sum(hit_table * logits[:, None, :], axis=-1))
    gates = jax.nn.softmax(picked, axis=-1)
    position, table = slot_table(routes)
    padded = jnp.concatenate([normed_two, jnp.zeros((1, D), jnp.float32)], axis=0)
    rows = low_back(padded[table // TOPK]).reshape(EXPERTS, CAP, D)
    gate_pre = low_back(jnp.einsum('ecd,edf->ecf', rows, gate_w, precision=HIGHEST))
    up_pre = low_back(jnp.einsum('ecd,edf->ecf', rows, up_w, precision=HIGHEST))
    hidden = low(jax.nn.silu(gate_pre) * up_pre)
    expert_out = low(low_back(jnp.einsum('ecf,efd->ecd', hidden, down_w, precision=HIGHEST)))
    per_choice = expert_out.reshape(EXPERTS * CAP, D)[position].reshape(length, TOPK, D)
    mixed = lax.optimization_barrier(jnp.sum(gates[:, :, None] * per_choice, axis=1))
    return middle + mixed

def reference(hidden_in, norm1_gain, w_query, w_key, w_value, w_out, norm2_gain, w_router, w_gate, w_up, w_down, expert_ids, out_grad):
    params = tuple((weight.astype(jnp.float32) for weight in (norm1_gain, w_query, w_key, w_value, w_out, norm2_gain, w_router, w_gate, w_up, w_down)))
    sequences = hidden_in.astype(jnp.float32).reshape(-1, TOK_DEV, D)
    routes_all = expert_ids.reshape(-1, TOK_DEV, TOPK)
    checked = jax.checkpoint(layer)

    def forward(inputs, *weights):

        def advance(carry, item):
            return (carry, checked(item[0], *weights, item[1]))
        return lax.scan(advance, jnp.zeros((), jnp.float32), (inputs, routes_all))[1]
    outputs, pullback = jax.vjp(forward, sequences, *params)
    grads = pullback(out_grad.astype(jnp.float32).reshape(-1, TOK_DEV, D))
    return (outputs.reshape(-1, D).astype(jnp.bfloat16), grads[0].reshape(-1, D).astype(jnp.bfloat16), grads[1], grads[2], grads[3], grads[4], grads[5], grads[6], grads[7], grads[8], grads[9], grads[10])
```

```python
import math

import jax
import jax.numpy as jnp
from jax import lax
from jax.sharding import PartitionSpec as P

HEADS = 16
KV_HEADS = 8
HEAD_DIM = 64
EXPERTS = 32
CAP = 152


EPSILON = 1e-06


def rope_tables(length, head_width):
    half_width = head_width // 2
    ladder = jnp.arange(half_width, dtype=jnp.float32) * (2.0 / head_width)
    inverse = jnp.exp(-math.log(10000.0) * ladder)
    angles = jnp.arange(length, dtype=jnp.float32)[:, None] * inverse[None, :]
    return (jnp.cos(angles), jnp.sin(angles))


def rotate(values, cosine, sine_table):
    half_width = values.shape[-1] // 2
    first_half = values[..., :half_width]
    second = values[..., half_width:]
    cos_rows = cosine[:, None, :]
    sin_rows = sine_table[:, None, :]
    return jnp.concatenate(
        [first_half * cos_rows - second * sin_rows, second * cos_rows + first_half * sin_rows],
        axis=-1,
    )


def unrotate(grads, cosine, sine_table):
    half_width = grads.shape[-1] // 2
    first_half = grads[..., :half_width]
    second = grads[..., half_width:]
    cos_rows = cosine[:, None, :]
    sin_rows = sine_table[:, None, :]
    return jnp.concatenate(
        [first_half * cos_rows + second * sin_rows, second * cos_rows - first_half * sin_rows],
        axis=-1,
    )


def shift(array, axis, step):
    count = lax.axis_size(axis)
    return lax.ppermute(array, axis, [(i, (i + step) % count) for i in range(count)])


def take_rows(array, start, rows):
    return lax.dynamic_slice_in_dim(array, start, rows, axis=0)


def block_scores(query_block, keys, start, scale):
    scores = (
        jnp.einsum("qgrd,kgd->grqk", query_block, keys, preferred_element_type=jnp.float32) * scale
    )
    query_pos = start + jnp.arange(query_block.shape[0], dtype=jnp.int32)
    key_pos = jnp.arange(keys.shape[0], dtype=jnp.int32)
    return jnp.where(key_pos[None, :] <= query_pos[:, None], scores, -1e30)


def local(
    hidden_in,
    norm1_gain,
    w_query,
    w_key,
    w_value,
    w_out,
    norm2_gain,
    w_router,
    w_gate,
    w_up,
    w_down,
    expert_ids,
    out_grad,
):
    owners = lax.axis_size("expert")
    me = lax.axis_index("expert")
    local_experts = EXPERTS // owners
    experts = jnp.arange(EXPERTS, dtype=jnp.int32)
    mask = jnp.sum((expert_ids[:, :, None] == experts[None, None, :]).astype(jnp.float32), axis=1)
    shard = w_query.shape[0]
    tail = jnp.concatenate(
        [
            w_router,
            norm1_gain[:, None],
            norm2_gain[:, None],
            jnp.zeros((shard, 128 - EXPERTS - 2), jnp.bfloat16),
        ],
        axis=1,
    )
    dense = lax.all_gather(
        jnp.concatenate([w_query, w_key, w_value, w_out, tail], axis=1),
        ("dp", "expert"),
        axis=0,
        tiled=True,
    )
    q_end = HEADS * HEAD_DIM
    k_end = q_end + KV_HEADS * HEAD_DIM
    v_end = k_end + KV_HEADS * HEAD_DIM
    o_end = v_end + w_out.shape[1]
    qkv_w = dense[:, :v_end]
    out_w = dense[:, v_end:o_end]
    router_w = dense[:, o_end : o_end + EXPERTS]
    gain_one = dense[:, o_end + EXPERTS]
    gain_two = dense[:, o_end + EXPERTS + 1]
    down_shard = jnp.swapaxes(w_down, 1, 2)
    gate_w = lax.all_gather(w_gate, "dp", axis=1, tiled=True)
    up_w = lax.all_gather(w_up, "dp", axis=1, tiled=True)
    down_w = lax.all_gather(down_shard, "dp", axis=1, tiled=True)
    early = jnp.concatenate(
        [
            out_grad,
            mask.astype(jnp.bfloat16),
            jnp.zeros((mask.shape[0], 128 - EXPERTS), jnp.bfloat16),
        ],
        axis=1,
    )
    early_all = jnp.stack([early] + [shift(early, "expert", r) for r in range(1, owners)])
    inputs = hidden_in.astype(jnp.float32)
    length = inputs.shape[0]
    width = inputs.shape[1]
    group = HEADS // KV_HEADS
    scale = 1.0 / math.sqrt(HEAD_DIM)
    block_rows = min(512, length)
    cosine, sine_table = rope_tables(length, HEAD_DIM)
    factor_one = lax.rsqrt(jnp.mean(inputs * inputs, axis=-1, keepdims=True) + EPSILON)
    scaled_one = inputs * factor_one
    normed = (scaled_one * gain_one.astype(jnp.float32)).astype(jnp.bfloat16)
    qkv = jnp.dot(normed, qkv_w, preferred_element_type=jnp.float32)
    queries = qkv[:, :q_end].reshape(length, HEADS, HEAD_DIM)
    keys = qkv[:, q_end:k_end].reshape(length, KV_HEADS, HEAD_DIM)
    values_in = qkv[:, k_end:].astype(jnp.bfloat16).reshape(length, KV_HEADS, HEAD_DIM)
    queries = (
        rotate(queries, cosine, sine_table)
        .astype(jnp.bfloat16)
        .reshape(length, KV_HEADS, group, HEAD_DIM)
    )
    keys = rotate(keys, cosine, sine_table).astype(jnp.bfloat16)
    block_index = 0
    start = block_index * block_rows
    scores = block_scores(queries, keys, start, scale)
    top_score = jnp.max(scores, axis=-1, keepdims=True)
    log_total = top_score + jnp.log(jnp.sum(jnp.exp(scores - top_score), axis=-1, keepdims=True))
    weights = jnp.exp(scores - log_total).astype(jnp.bfloat16)
    pieces = jnp.einsum("grqk,kgd->qgrd", weights, values_in, preferred_element_type=jnp.float32)
    log_totals = [log_total]
    attended = pieces.reshape(length, HEADS * HEAD_DIM).astype(jnp.bfloat16)
    middle = inputs + jnp.dot(attended, out_w, preferred_element_type=jnp.float32)
    factor_two = lax.rsqrt(jnp.mean(middle * middle, axis=-1, keepdims=True) + EPSILON)
    scaled_two = middle * factor_two
    gain_float = gain_two.astype(jnp.float32)
    normed_two = (scaled_two * gain_float).astype(jnp.bfloat16)
    tokens = jnp.stack([normed_two] + [shift(normed_two, "expert", r) for r in range(1, owners)])
    grads_all = early_all[:, :, :width]
    mask_bf = early_all[:, :, width : width + EXPERTS]
    mask_all = mask_bf.astype(jnp.float32)
    order = jnp.arange(length, dtype=jnp.int32)
    before = (order[:, None] > order[None, :]).astype(jnp.bfloat16)
    mask_own = lax.dynamic_slice_in_dim(mask_bf, me * local_experts, local_experts, axis=2)
    ranks = jnp.einsum("stj,ut->sju", mask_own, before, preferred_element_type=jnp.float32)
    slots = jnp.where(
        jnp.swapaxes(mask_own, 1, 2) > 0, ranks.astype(jnp.int32), -1
    )
    places = slots[:, :, None, :] == jnp.arange(CAP, dtype=jnp.int32)[None, None, :, None]
    picks = places.astype(jnp.bfloat16)
    logits = jnp.einsum("std,de->ste", tokens, router_w, preferred_element_type=jnp.float32)
    masked = jnp.where(mask_all > 0, logits, -jnp.inf)
    raised = jnp.exp(masked - jnp.max(masked, axis=-1, keepdims=True))
    gates_all = raised / jnp.sum(raised, axis=-1, keepdims=True)
    gates = gates_all[0]
    gates_own = jnp.swapaxes(
        lax.dynamic_slice_in_dim(gates_all, me * local_experts, local_experts, axis=2), 1, 2
    )
    gate_slot = jnp.sum(jnp.where(places, gates_own[:, :, None, :], 0.0), axis=-1)
    grad_rows = jnp.einsum(
        "sjct,std->sjcd", picks, grads_all, preferred_element_type=jnp.float32
    ).astype(jnp.bfloat16)
    rows = jnp.einsum(
        "sjct,std->sjcd", picks, tokens, preferred_element_type=jnp.float32
    ).astype(jnp.bfloat16)
    gate_pre = jnp.einsum("sjcd,jdf->sjcf", rows, gate_w, preferred_element_type=jnp.float32)
    up_pre = jnp.einsum("sjcd,jdf->sjcf", rows, up_w, preferred_element_type=jnp.float32)
    sigmoid_gate = jax.nn.sigmoid(gate_pre)
    activated = gate_pre * sigmoid_gate
    hidden = (activated * up_pre).astype(jnp.bfloat16)
    arrived = (gate_slot[..., None] * grad_rows.astype(jnp.float32)).astype(jnp.bfloat16)
    down_grad = jnp.einsum("sjcd,sjcf->jdf", arrived, hidden, preferred_element_type=jnp.float32)
    down_total = lax.psum_scatter(
        down_grad.astype(jnp.bfloat16), "dp", scatter_dimension=1, tiled=True
    )
    result = jnp.einsum(
        "sjcf,jdf->sjcd", hidden, down_w, preferred_element_type=jnp.float32
    ).astype(jnp.bfloat16)
    result_float = result.astype(jnp.float32)
    weighted = (gate_slot[..., None] * result_float).astype(jnp.bfloat16)
    mixed_parts = jnp.einsum("sjct,sjcd->std", picks, weighted, preferred_element_type=jnp.float32)
    slot_grads = jnp.sum(grad_rows.astype(jnp.float32) * result_float, axis=-1)
    gate_grad_parts = jnp.sum(jnp.where(places, slot_grads[..., None], 0.0), axis=2)
    mixed = mixed_parts[0]
    gate_pieces = [gate_grad_parts[0]]
    for r in range(1, owners):
        mixed = mixed + shift(mixed_parts[r].astype(jnp.bfloat16), "expert", -r).astype(
            jnp.float32
        )
        gate_pieces.append(shift(gate_grad_parts[r], "expert", -r))
    layer_out = (middle + mixed).astype(jnp.bfloat16)
    gate_grads = jnp.roll(jnp.stack(gate_pieces), me, axis=0).reshape(EXPERTS, length).T
    upstream = out_grad.astype(jnp.float32)
    logit_grads = gates * (gate_grads - jnp.sum(gates * gate_grads, axis=-1, keepdims=True))
    logit_grads = logit_grads.astype(jnp.bfloat16)
    router_grad = jnp.einsum(
        "td,te->de", normed_two, logit_grads, preferred_element_type=jnp.float32
    )
    normed_grad = jnp.einsum("te,de->td", logit_grads, router_w, preferred_element_type=jnp.float32)
    hidden_grad = jnp.einsum("sjcd,jdf->sjcf", arrived, down_w, preferred_element_type=jnp.float32)
    gate_pre_grad = (
        hidden_grad * up_pre * sigmoid_gate * (1.0 + gate_pre * (1.0 - sigmoid_gate))
    ).astype(jnp.bfloat16)
    up_pre_grad = (hidden_grad * activated).astype(jnp.bfloat16)
    row_grads = jnp.einsum(
        "sjcf,jdf->sjcd", gate_pre_grad, gate_w, preferred_element_type=jnp.float32
    )
    row_grads = (
        row_grads
        + jnp.einsum("sjcf,jdf->sjcd", up_pre_grad, up_w, preferred_element_type=jnp.float32)
    ).astype(jnp.bfloat16)
    back_parts = jnp.einsum("sjct,sjcd->std", picks, row_grads, preferred_element_type=jnp.float32)
    gate_grad = jnp.einsum(
        "sjcd,sjcf->jdf", rows, gate_pre_grad, preferred_element_type=jnp.float32
    )
    up_grad = jnp.einsum("sjcd,sjcf->jdf", rows, up_pre_grad, preferred_element_type=jnp.float32)
    gate_total = lax.psum_scatter(
        gate_grad.astype(jnp.bfloat16), "dp", scatter_dimension=1, tiled=True
    ).astype(jnp.float32)
    up_total = lax.psum_scatter(
        up_grad.astype(jnp.bfloat16), "dp", scatter_dimension=1, tiled=True
    ).astype(jnp.float32)
    down_total = jnp.swapaxes(down_total.astype(jnp.float32), 1, 2)
    normed_grad = normed_grad + back_parts[0]
    for r in range(1, owners):
        normed_grad = normed_grad + shift(
            back_parts[r].astype(jnp.bfloat16), "expert", -r
        ).astype(jnp.float32)
    gain_two_grad = jnp.sum(normed_grad * scaled_two, axis=0)
    scaled_grad = normed_grad * gain_float
    middle_grad = upstream + factor_two * (
        scaled_grad - scaled_two * jnp.mean(scaled_grad * scaled_two, axis=-1, keepdims=True)
    )
    branch_grad = middle_grad.astype(jnp.bfloat16)
    out_w_grad = jnp.einsum("tk,td->kd", attended, branch_grad, preferred_element_type=jnp.float32)
    attended_grad = jnp.einsum(
        "td,kd->tk", branch_grad, out_w, preferred_element_type=jnp.float32
    ).astype(jnp.bfloat16)
    attended_grad = attended_grad.reshape(length, KV_HEADS, group, HEAD_DIM)
    key_grads = jnp.zeros((length, KV_HEADS, HEAD_DIM), jnp.float32)
    value_grads = jnp.zeros((length, KV_HEADS, HEAD_DIM), jnp.float32)
    block_index = 0
    start = block_index * block_rows
    key_len = start + block_rows
    scores = block_scores(queries, keys, start, scale)
    weights = jnp.exp(scores - log_totals[block_index])
    value_grads = value_grads.at[:key_len].add(
        jnp.einsum(
            "grqk,qgrd->kgd",
            weights.astype(jnp.bfloat16),
            attended_grad,
            preferred_element_type=jnp.float32,
        )
    )
    weight_grads = jnp.einsum(
        "qgrd,kgd->grqk", attended_grad, values_in, preferred_element_type=jnp.float32
    )
    centre = jnp.sum(weights * weight_grads, axis=-1, keepdims=True)
    score_grads = (weights * (weight_grads - centre)).astype(jnp.bfloat16)
    query_pieces = (
        jnp.einsum("grqk,kgd->qgrd", score_grads, keys, preferred_element_type=jnp.float32) * scale
    )
    key_grads = key_grads.at[:key_len].add(
        jnp.einsum("grqk,qgrd->kgd", score_grads, queries, preferred_element_type=jnp.float32)
        * scale
    )
    query_grads = query_pieces.reshape(length, HEADS, HEAD_DIM)
    query_grads = (
        unrotate(query_grads, cosine, sine_table)
        .reshape(length, HEADS * HEAD_DIM)
        .astype(jnp.bfloat16)
    )
    key_grads = (
        unrotate(key_grads, cosine, sine_table)
        .reshape(length, KV_HEADS * HEAD_DIM)
        .astype(jnp.bfloat16)
    )
    value_grads = value_grads.reshape(length, KV_HEADS * HEAD_DIM).astype(jnp.bfloat16)
    qkv_grads = jnp.concatenate([query_grads, key_grads, value_grads], axis=1)
    qkv_w_grad = jnp.einsum("td,tk->dk", normed, qkv_grads, preferred_element_type=jnp.float32)
    first_grad = jnp.einsum("tk,dk->td", qkv_grads, qkv_w, preferred_element_type=jnp.float32)
    gain_one_grad = jnp.sum(first_grad * scaled_one, axis=0)
    scaled_one_grad = first_grad * gain_one.astype(jnp.float32)
    input_grad = middle_grad + factor_one * (
        scaled_one_grad
        - scaled_one * jnp.mean(scaled_one_grad * scaled_one, axis=-1, keepdims=True)
    )
    tail_grad = jnp.concatenate(
        [
            router_grad,
            gain_one_grad[:, None],
            gain_two_grad[:, None],
            jnp.zeros((width, 128 - EXPERTS - 2), jnp.float32),
        ],
        axis=1,
    )
    dense_grad = jnp.concatenate(
        [
            qkv_w_grad.astype(jnp.bfloat16),
            out_w_grad.astype(jnp.bfloat16),
            tail_grad.astype(jnp.bfloat16),
        ],
        axis=1,
    )
    dense_part = lax.psum_scatter(dense_grad, "dp", scatter_dimension=0, tiled=True)
    total = take_rows(dense_part, me * shard, shard).astype(jnp.float32)
    for r in range(1, owners):
        piece = take_rows(dense_part, lax.rem(me + r, owners) * shard, shard)
        total = total + shift(piece, "expert", r).astype(jnp.float32)
    return (
        layer_out,
        input_grad.astype(jnp.bfloat16),
        total[:, o_end + EXPERTS],
        total[:, :q_end],
        total[:, q_end:k_end],
        total[:, k_end:v_end],
        total[:, v_end:o_end],
        total[:, o_end + EXPERTS + 1],
        total[:, o_end : o_end + EXPERTS],
        gate_total,
        up_total,
        down_total,
    )


def solution(mesh):
    return jax.shard_map(
        local,
        mesh=mesh,
        in_specs=(
            P(("dp", "expert"), None),
            P(("dp", "expert")),
            P(("dp", "expert"), None),
            P(("dp", "expert"), None),
            P(("dp", "expert"), None),
            P(("dp", "expert"), None),
            P(("dp", "expert")),
            P(("dp", "expert"), None),
            P("expert", "dp", None),
            P("expert", "dp", None),
            P("expert", None, "dp"),
            P(("dp", "expert"), None),
            P(("dp", "expert"), None),
        ),
        out_specs=(
            P(("dp", "expert"), None),
            P(("dp", "expert"), None),
            P(("dp", "expert")),
            P(("dp", "expert"), None),
            P(("dp", "expert"), None),
            P(("dp", "expert"), None),
            P(("dp", "expert"), None),
            P(("dp", "expert")),
            P(("dp", "expert"), None),
            P("expert", "dp", None),
            P("expert", "dp", None),
            P("expert", None, "dp"),
        ),
        check_vma=False,
    )
```

```python
import math

import jax
import jax.numpy as jnp
from jax import lax
from jax.experimental.layout import Layout, with_layout_constraint
from jax.sharding import PartitionSpec as P

HEADS = 16
KV_HEADS = 8
HEAD_DIM = 64
EXPERTS = 32
CAP = 152


EPSILON = 1e-06


def rope_tables(length, head_width):
    half_width = head_width // 2
    ladder = jnp.arange(half_width, dtype=jnp.float32) * (2.0 / head_width)
    inverse = jnp.exp(-math.log(10000.0) * ladder)
    angles = jnp.arange(length, dtype=jnp.float32)[:, None] * inverse[None, :]
    return (jnp.cos(angles), jnp.sin(angles))


def rotate(values, cosine, sine_table):
    half_width = values.shape[-1] // 2
    first_half = values[..., :half_width]
    second = values[..., half_width:]
    cos_rows = cosine[:, None, :]
    sin_rows = sine_table[:, None, :]
    return jnp.concatenate(
        [first_half * cos_rows - second * sin_rows, second * cos_rows + first_half * sin_rows],
        axis=-1,
    )


def unrotate(grads, cosine, sine_table):
    half_width = grads.shape[-1] // 2
    first_half = grads[..., :half_width]
    second = grads[..., half_width:]
    cos_rows = cosine[:, None, :]
    sin_rows = sine_table[:, None, :]
    return jnp.concatenate(
        [first_half * cos_rows + second * sin_rows, second * cos_rows - first_half * sin_rows],
        axis=-1,
    )


def shift(array, axis, step):
    count = lax.axis_size(axis)
    return lax.ppermute(array, axis, [(i, (i + step) % count) for i in range(count)])


def row_major(array):
    return with_layout_constraint(array, Layout(major_to_minor=tuple(range(array.ndim))))


def take_rows(array, start, rows):
    return lax.dynamic_slice_in_dim(array, start, rows, axis=0)


def block_scores(query_block, keys, start, scale):
    scores = (
        jnp.einsum("qgrd,kgd->grqk", query_block, keys, preferred_element_type=jnp.float32) * scale
    )
    query_pos = start + jnp.arange(query_block.shape[0], dtype=jnp.int32)
    key_pos = jnp.arange(keys.shape[0], dtype=jnp.int32)
    return jnp.where(key_pos[None, :] <= query_pos[:, None], scores, -1e30)


def local(
    hidden_in,
    norm1_gain,
    w_query,
    w_key,
    w_value,
    w_out,
    norm2_gain,
    w_router,
    w_gate,
    w_up,
    w_down,
    expert_ids,
    out_grad,
):
    owners = lax.axis_size("expert")
    me = lax.axis_index("expert")
    local_experts = EXPERTS // owners
    experts = jnp.arange(EXPERTS, dtype=jnp.int32)
    mask = jnp.sum((expert_ids[:, :, None] == experts[None, None, :]).astype(jnp.float32), axis=1)
    shard = w_query.shape[0]
    tail = jnp.concatenate(
        [
            w_router,
            norm1_gain[:, None],
            norm2_gain[:, None],
            jnp.zeros((shard, 128 - EXPERTS - 2), jnp.bfloat16),
        ],
        axis=1,
    )
    dense_shard = jnp.concatenate([w_query, w_key, w_value, w_out, tail], axis=1)
    dense_near = jnp.stack(
        [dense_shard] + [shift(dense_shard, "expert", -r) for r in range(1, owners)]
    )
    dense_near = jnp.roll(dense_near, me, axis=0).reshape(owners * shard, -1)
    q_end = HEADS * HEAD_DIM
    k_end = q_end + KV_HEADS * HEAD_DIM
    v_end = k_end + KV_HEADS * HEAD_DIM
    o_end = v_end + w_out.shape[1]
    down_shard = jnp.swapaxes(w_down, 1, 2)
    early = jnp.concatenate(
        [
            out_grad,
            mask.astype(jnp.bfloat16),
            jnp.zeros((mask.shape[0], 128 - EXPERTS), jnp.bfloat16),
        ],
        axis=1,
    )
    early, dense_near, w_gate, w_up, down_shard = lax.optimization_barrier(
        (early, dense_near, w_gate, w_up, down_shard)
    )
    dense = row_major(lax.all_gather(row_major(dense_near), "dp", axis=0, tiled=True))
    early = row_major(early)
    gate_w = lax.all_gather(w_gate, "dp", axis=1, tiled=True)
    up_w = lax.all_gather(w_up, "dp", axis=1, tiled=True)
    down_w = lax.all_gather(down_shard, "dp", axis=1, tiled=True)
    qkv_w = dense[:, :v_end]
    out_w = dense[:, v_end:o_end]
    router_w = dense[:, o_end : o_end + EXPERTS]
    gain_one = dense[:, o_end + EXPERTS]
    gain_two = dense[:, o_end + EXPERTS + 1]
    early_all = row_major(
        jnp.stack([early] + [shift(early, "expert", r) for r in range(1, owners)])
    )
    inputs = hidden_in.astype(jnp.float32)
    length = inputs.shape[0]
    width = inputs.shape[1]
    group = HEADS // KV_HEADS
    scale = 1.0 / math.sqrt(HEAD_DIM)
    block_rows = min(512, length)
    cosine, sine_table = rope_tables(length, HEAD_DIM)
    factor_one = lax.rsqrt(jnp.mean(inputs * inputs, axis=-1, keepdims=True) + EPSILON)
    scaled_one = inputs * factor_one
    normed = (scaled_one * gain_one.astype(jnp.float32)).astype(jnp.bfloat16)
    qkv = jnp.dot(normed, qkv_w, preferred_element_type=jnp.float32)
    queries = qkv[:, :q_end].reshape(length, HEADS, HEAD_DIM)
    keys = qkv[:, q_end:k_end].reshape(length, KV_HEADS, HEAD_DIM)
    values_in = qkv[:, k_end:].astype(jnp.bfloat16).reshape(length, KV_HEADS, HEAD_DIM)
    queries = (
        rotate(queries, cosine, sine_table)
        .astype(jnp.bfloat16)
        .reshape(length, KV_HEADS, group, HEAD_DIM)
    )
    keys = rotate(keys, cosine, sine_table).astype(jnp.bfloat16)
    block_index = 0
    start = block_index * block_rows
    scores = block_scores(queries, keys, start, scale)
    top_score = jnp.max(scores, axis=-1, keepdims=True)
    log_total = top_score + jnp.log(jnp.sum(jnp.exp(scores - top_score), axis=-1, keepdims=True))
    weights = jnp.exp(scores - log_total).astype(jnp.bfloat16)
    pieces = jnp.einsum("grqk,kgd->qgrd", weights, values_in, preferred_element_type=jnp.float32)
    log_totals = [log_total]
    attended = pieces.reshape(length, HEADS * HEAD_DIM).astype(jnp.bfloat16)
    middle = inputs + jnp.dot(attended, out_w, preferred_element_type=jnp.float32)
    factor_two = lax.rsqrt(jnp.mean(middle * middle, axis=-1, keepdims=True) + EPSILON)
    scaled_two = middle * factor_two
    gain_float = gain_two.astype(jnp.float32)
    normed_two = (scaled_two * gain_float).astype(jnp.bfloat16)
    tokens = jnp.stack([normed_two] + [shift(normed_two, "expert", r) for r in range(1, owners)])
    grads_all = early_all[:, :, :width]
    mask_bf = early_all[:, :, width : width + EXPERTS]
    mask_all = mask_bf.astype(jnp.float32)
    order = jnp.arange(length, dtype=jnp.int32)
    before = (order[:, None] > order[None, :]).astype(jnp.bfloat16)
    mask_own = lax.dynamic_slice_in_dim(mask_bf, me * local_experts, local_experts, axis=2)
    ranks = jnp.einsum("stj,ut->sju", mask_own, before, preferred_element_type=jnp.float32)
    slots = jnp.where(
        jnp.swapaxes(mask_own, 1, 2) > 0, ranks.astype(jnp.int32), -1
    )
    places = slots[:, :, None, :] == jnp.arange(CAP, dtype=jnp.int32)[None, None, :, None]
    picks = places.astype(jnp.bfloat16)
    logits = jnp.einsum("std,de->ste", tokens, router_w, preferred_element_type=jnp.float32)
    masked = jnp.where(mask_all > 0, logits, -jnp.inf)
    raised = jnp.exp(masked - jnp.max(masked, axis=-1, keepdims=True))
    gates_all = raised / jnp.sum(raised, axis=-1, keepdims=True)
    gates = gates_all[0]
    gates_own = jnp.swapaxes(
        lax.dynamic_slice_in_dim(gates_all, me * local_experts, local_experts, axis=2), 1, 2
    )
    gate_slot = jnp.sum(jnp.where(places, gates_own[:, :, None, :], 0.0), axis=-1)
    grad_rows = jnp.einsum(
        "sjct,std->sjcd", picks, grads_all, preferred_element_type=jnp.float32
    ).astype(jnp.bfloat16)
    rows = jnp.einsum(
        "sjct,std->sjcd", picks, tokens, preferred_element_type=jnp.float32
    ).astype(jnp.bfloat16)
    gate_pre = jnp.einsum("sjcd,jdf->sjcf", rows, gate_w, preferred_element_type=jnp.float32)
    up_pre = jnp.einsum("sjcd,jdf->sjcf", rows, up_w, preferred_element_type=jnp.float32)
    sigmoid_gate = jax.nn.sigmoid(gate_pre)
    activated = gate_pre * sigmoid_gate
    hidden = (activated * up_pre).astype(jnp.bfloat16)
    arrived = (gate_slot[..., None] * grad_rows.astype(jnp.float32)).astype(jnp.bfloat16)
    down_grad = jnp.einsum("sjcd,sjcf->jdf", arrived, hidden, preferred_element_type=jnp.float32)
    result = jnp.einsum(
        "sjcf,jdf->sjcd", hidden, down_w, preferred_element_type=jnp.float32
    ).astype(jnp.bfloat16)
    result_float = result.astype(jnp.float32)
    weighted = (gate_slot[..., None] * result_float).astype(jnp.bfloat16)
    mixed_parts = jnp.einsum("sjct,sjcd->std", picks, weighted, preferred_element_type=jnp.float32)
    slot_grads = jnp.sum(grad_rows.astype(jnp.float32) * result_float, axis=-1)
    gate_grad_parts = jnp.sum(jnp.where(places, slot_grads[..., None], 0.0), axis=2)
    mixed = middle + mixed_parts[0]
    mixed_away = mixed_parts[1:].astype(jnp.bfloat16)
    gate_pieces = [gate_grad_parts[0]]
    for r in range(1, owners):
        gate_pieces.append(shift(gate_grad_parts[r], "expert", -r))
    gate_grads = jnp.roll(jnp.stack(gate_pieces), me, axis=0).reshape(EXPERTS, length).T
    upstream = out_grad.astype(jnp.float32)
    logit_grads = gates * (gate_grads - jnp.sum(gates * gate_grads, axis=-1, keepdims=True))
    logit_grads = logit_grads.astype(jnp.bfloat16)
    router_grad = jnp.einsum(
        "td,te->de", normed_two, logit_grads, preferred_element_type=jnp.float32
    )
    normed_grad = jnp.einsum("te,de->td", logit_grads, router_w, preferred_element_type=jnp.float32)
    hidden_grad = jnp.einsum("sjcd,jdf->sjcf", arrived, down_w, preferred_element_type=jnp.float32)
    gate_pre_grad = (
        hidden_grad * up_pre * sigmoid_gate * (1.0 + gate_pre * (1.0 - sigmoid_gate))
    ).astype(jnp.bfloat16)
    up_pre_grad = (hidden_grad * activated).astype(jnp.bfloat16)
    down_grad = down_grad.astype(jnp.bfloat16)
    gate_grad = jnp.einsum(
        "sjcd,sjcf->jdf", rows, gate_pre_grad, preferred_element_type=jnp.float32
    ).astype(jnp.bfloat16)
    gate_pre_grad, up_pre_grad, down_grad = lax.optimization_barrier(
        (gate_pre_grad, up_pre_grad, down_grad)
    )
    down_total = lax.psum_scatter(down_grad, "dp", scatter_dimension=1, tiled=True)
    row_grads = jnp.einsum(
        "sjcf,jdf->sjcd", gate_pre_grad, gate_w, preferred_element_type=jnp.float32
    )
    row_grads = (
        row_grads
        + jnp.einsum("sjcf,jdf->sjcd", up_pre_grad, up_w, preferred_element_type=jnp.float32)
    ).astype(jnp.bfloat16)
    back_parts = jnp.einsum("sjct,sjcd->std", picks, row_grads, preferred_element_type=jnp.float32)
    up_grad = jnp.einsum("sjcd,sjcf->jdf", rows, up_pre_grad, preferred_element_type=jnp.float32)
    gate_total = lax.psum_scatter(
        gate_grad, "dp", scatter_dimension=1, tiled=True
    )
    up_total = lax.psum_scatter(
        up_grad.astype(jnp.bfloat16), "dp", scatter_dimension=1, tiled=True
    )
    normed_grad = normed_grad + back_parts[0]
    for r in range(1, owners):
        normed_grad = normed_grad + shift(
            back_parts[r].astype(jnp.bfloat16), "expert", -r
        ).astype(jnp.float32)
    normed_grad, mixed_away, down_total = lax.optimization_barrier(
        (normed_grad, mixed_away, down_total)
    )
    mixed_home = [shift(mixed_away[r - 1], "expert", -r) for r in range(1, owners)]
    gain_two_grad = jnp.sum(normed_grad * scaled_two, axis=0)
    scaled_grad = normed_grad * gain_float
    middle_grad = upstream + factor_two * (
        scaled_grad - scaled_two * jnp.mean(scaled_grad * scaled_two, axis=-1, keepdims=True)
    )
    branch_grad = middle_grad.astype(jnp.bfloat16)
    out_w_grad = jnp.einsum("tk,td->kd", attended, branch_grad, preferred_element_type=jnp.float32)
    attended_grad = jnp.einsum(
        "td,kd->tk", branch_grad, out_w, preferred_element_type=jnp.float32
    ).astype(jnp.bfloat16)
    attended_grad = attended_grad.reshape(length, KV_HEADS, group, HEAD_DIM)
    key_grads = jnp.zeros((length, KV_HEADS, HEAD_DIM), jnp.float32)
    value_grads = jnp.zeros((length, KV_HEADS, HEAD_DIM), jnp.float32)
    block_index = 0
    start = block_index * block_rows
    key_len = start + block_rows
    scores = block_scores(queries, keys, start, scale)
    weights = jnp.exp(scores - log_totals[block_index])
    value_grads = value_grads.at[:key_len].add(
        jnp.einsum(
            "grqk,qgrd->kgd",
            weights.astype(jnp.bfloat16),
            attended_grad,
            preferred_element_type=jnp.float32,
        )
    )
    weight_grads = jnp.einsum(
        "qgrd,kgd->grqk", attended_grad, values_in, preferred_element_type=jnp.float32
    )
    centre = jnp.sum(weights * weight_grads, axis=-1, keepdims=True)
    score_grads = (weights * (weight_grads - centre)).astype(jnp.bfloat16)
    query_pieces = (
        jnp.einsum("grqk,kgd->qgrd", score_grads, keys, preferred_element_type=jnp.float32) * scale
    )
    key_grads = key_grads.at[:key_len].add(
        jnp.einsum("grqk,qgrd->kgd", score_grads, queries, preferred_element_type=jnp.float32)
        * scale
    )
    query_grads = query_pieces.reshape(length, HEADS, HEAD_DIM)
    query_grads = (
        unrotate(query_grads, cosine, sine_table)
        .reshape(length, HEADS * HEAD_DIM)
        .astype(jnp.bfloat16)
    )
    key_grads = (
        unrotate(key_grads, cosine, sine_table)
        .reshape(length, KV_HEADS * HEAD_DIM)
        .astype(jnp.bfloat16)
    )
    value_grads = value_grads.reshape(length, KV_HEADS * HEAD_DIM).astype(jnp.bfloat16)
    qkv_grads = jnp.concatenate([query_grads, key_grads, value_grads], axis=1)
    qkv_w_grad = jnp.einsum("td,tk->dk", normed, qkv_grads, preferred_element_type=jnp.float32)
    first_grad = jnp.einsum("tk,dk->td", qkv_grads, qkv_w, preferred_element_type=jnp.float32)
    gain_one_grad = jnp.sum(first_grad * scaled_one, axis=0)
    scaled_one_grad = first_grad * gain_one.astype(jnp.float32)
    input_grad = middle_grad + factor_one * (
        scaled_one_grad
        - scaled_one * jnp.mean(scaled_one_grad * scaled_one, axis=-1, keepdims=True)
    )
    tail_grad = jnp.concatenate(
        [
            router_grad,
            gain_one_grad[:, None],
            gain_two_grad[:, None],
            jnp.zeros((width, 128 - EXPERTS - 2), jnp.float32),
        ],
        axis=1,
    )
    dense_grad = jnp.concatenate(
        [
            qkv_w_grad.astype(jnp.bfloat16),
            out_w_grad.astype(jnp.bfloat16),
            tail_grad.astype(jnp.bfloat16),
        ],
        axis=1,
    )
    dense_grad, gate_total, up_total, mixed_home = lax.optimization_barrier(
        (dense_grad, gate_total, up_total, mixed_home)
    )
    for piece in mixed_home:
        mixed = mixed + piece.astype(jnp.float32)
    layer_out = mixed.astype(jnp.bfloat16)
    dense_part = lax.psum_scatter(dense_grad, "dp", scatter_dimension=0, tiled=True)
    total = take_rows(dense_part, me * shard, shard).astype(jnp.float32)
    for r in range(1, owners):
        piece = take_rows(dense_part, lax.rem(me + r, owners) * shard, shard)
        total = total + shift(piece, "expert", r).astype(jnp.float32)
    return (
        layer_out,
        input_grad.astype(jnp.bfloat16),
        total[:, o_end + EXPERTS],
        total[:, :q_end],
        total[:, q_end:k_end],
        total[:, k_end:v_end],
        total[:, v_end:o_end],
        total[:, o_end + EXPERTS + 1],
        total[:, o_end : o_end + EXPERTS],
        gate_total.astype(jnp.float32),
        up_total.astype(jnp.float32),
        jnp.swapaxes(down_total.astype(jnp.float32), 1, 2),
    )


def solution(mesh):
    return jax.shard_map(
        local,
        mesh=mesh,
        in_specs=(
            P(("dp", "expert"), None),
            P(("dp", "expert")),
            P(("dp", "expert"), None),
            P(("dp", "expert"), None),
            P(("dp", "expert"), None),
            P(("dp", "expert"), None),
            P(("dp", "expert")),
            P(("dp", "expert"), None),
            P("expert", "dp", None),
            P("expert", "dp", None),
            P("expert", None, "dp"),
            P(("dp", "expert"), None),
            P(("dp", "expert"), None),
        ),
        out_specs=(
            P(("dp", "expert"), None),
            P(("dp", "expert"), None),
            P(("dp", "expert")),
            P(("dp", "expert"), None),
            P(("dp", "expert"), None),
            P(("dp", "expert"), None),
            P(("dp", "expert"), None),
            P(("dp", "expert")),
            P(("dp", "expert"), None),
            P("expert", "dp", None),
            P("expert", "dp", None),
            P("expert", None, "dp"),
        ),
        check_vma=False,
    )
```
